32 devices in a mesh: dp: 16 (over z, x, core), tensor: 2 (over y).
Axes of the slice: x: 2, y: 2, z: 4, core: 2. Of those that a mesh axis runs over, the one named last changes fastest.
Arguments:
- latents: float32 [128, 256, 1152], P('dp'), may hold values from -8 to 8
- cotangent: float32 [128, 256, 1152], P('dp'), may hold values from -8 to 8
- timesteps: int32 [128], P('dp'), may hold values from 0 to 999
- labels: int32 [128], P('dp'), may hold values from 0 to 1000
- label_table: float32 [1001, 1152], replicated, may hold values from -6 to 6
- modulate_w: float32 [1152, 6, 1152], P('dp', None, 'tensor'), may hold values from -0.1875 to 0.1875
- attend_w: float32 [1152, 3, 1152], P('dp', None, 'tensor'), may hold values from -0.1875 to 0.1875
- output_projection_weight: float32 [1152, 1152], P('tensor', 'dp'), may hold values from -0.75 to 0.75
- expand_w: float32 [1152, 4, 1152], P('dp', None, 'tensor'), may hold values from -0.1875 to 0.1875
- contract_w: float32 [4, 1152, 1152], P(None, 'tensor', 'dp'), may hold values from -0.09375 to 0.09375
- units_bias: float32 [12, 1152], P(None, 'tensor'), may hold values from -1.75 to 1.75
- output_width_bias: float32 [2, 1152], replicated, may hold values from -1.75 to 1.75
- modulate_mean: float32 [1152, 6, 1152], P('dp', None, 'tensor'), may hold values from -128 to 128
- modulate_square: float32 [1152, 6, 1152], P('dp', None, 'tensor'), may hold values from 45.8752 to 190.0544
- attend_mean: float32 [1152, 3, 1152], P('dp', None, 'tensor'), may hold values from -160 to 160
- attend_square: float32 [1152, 3, 1152], P('dp', None, 'tensor'), may hold values from 65.536 to 262.144
- project_mean: float32 [1152, 1152], P('tensor', 'dp'), may hold values from -48 to 48
- project_square: float32 [1152, 1152], P('tensor', 'dp'), may hold values from 5.24288 to 20.97152
- expand_mean: float32 [1152, 4, 1152], P('dp', None, 'tensor'), may hold values from -80 to 80
- expand_square: float32 [1152, 4, 1152], P('dp', None, 'tensor'), may hold values from 16.384 to 65.536
- contract_mean: float32 [4, 1152, 1152], P(None, 'tensor', 'dp'), may hold values from -64 to 64
- contract_square: float32 [4, 1152, 1152], P(None, 'tensor', 'dp'), may hold values from 11.79648 to 47.18592
- units_mean: float32 [12, 1152], P(None, 'tensor'), may hold values from -128 to 128
- units_square: float32 [12, 1152], P(None, 'tensor'), may hold values from 32.768 to 131.072
- widths_mean: float32 [2, 1152], replicated, may hold values from -128 to 128
- widths_square: float32 [2, 1152], replicated, may hold values from 32.768 to 131.072
Outputs:
- block_out: float32 [128, 256, 1152], P('dp')
- latents_grad: float32 [128, 256, 1152], P('dp')
- cond_grad: float32 [128, 1152], P('dp')
- modulate_grad: float32 [1152, 6, 1152], P('dp', None, 'tensor')
- modulate_moment: float32 [1152, 6, 1152], P('dp', None, 'tensor')
- modulate_second: float32 [1152, 6, 1152], P('dp', None, 'tensor')
- modulate_next: float32 [1152, 6, 1152], P('dp', None, 'tensor')
- attend_grad: float32 [1152, 3, 1152], P('dp', None, 'tensor')
- attend_moment: float32 [1152, 3, 1152], P('dp', None, 'tensor')
- attend_second: float32 [1152, 3, 1152], P('dp', None, 'tensor')
- attend_next: float32 [1152, 3, 1152], P('dp', None, 'tensor')
- project_grad: float32 [1152, 1152], P('tensor', 'dp')
- project_moment: float32 [1152, 1152], P('tensor', 'dp')
- project_second: float32 [1152, 1152], P('tensor', 'dp')
- project_next: float32 [1152, 1152], P('tensor', 'dp')
- expand_grad: float32 [1152, 4, 1152], P('dp', None, 'tensor')
- expand_moment: float32 [1152, 4, 1152], P('dp', None, 'tensor')
- expand_second: float32 [1152, 4, 1152], P('dp', None, 'tensor')
- expand_next: float32 [1152, 4, 1152], P('dp', None, 'tensor')
- contract_grad: float32 [4, 1152, 1152], P(None, 'tensor', 'dp')
- contract_moment: float32 [4, 1152, 1152], P(None, 'tensor', 'dp')
- contract_second: float32 [4, 1152, 1152], P(None, 'tensor', 'dp')
- contract_next: float32 [4, 1152, 1152], P(None, 'tensor', 'dp')
- units_grad: float32 [12, 1152], P(None, 'tensor')
- units_moment: float32 [12, 1152], P(None, 'tensor')
- units_second: float32 [12, 1152], P(None, 'tensor')
- units_next: float32 [12, 1152], P(None, 'tensor')
- widths_grad: float32 [2, 1152], replicated
- widths_moment: float32 [2, 1152], replicated
- widths_second: float32 [2, 1152], replicated
- widths_next: float32 [2, 1152], replicated
The draws below stay inside these ranges and needn't reach their ends.
All inputs are finite; a program needn't handle non-finite values.
Results may differ from the reference program's by a relative error of at most 0.017.
Values may be sent and summed in bfloat16 or wider, within the bound.
A program may use at most 320 MiB of HBM per device.

```python
import math
import jax
import jax.numpy as jnp
from jax import lax

D = 1152
HEADS = 16
HEAD_DIM = 72
FF = 4608
CLASSES = 1001
SEQ = 256
STEP = 10
BLOCKS = 4
BATCH = 128
TOKENS = 32768
N_DP = 16


def touch_ends(result, stream_key, low, high):
    spot = [jax.random.randint(jax.random.fold_in(stream_key, axis), (), 0, length) for axis, length in enumerate(result.shape)]
    longest = result.shape.index(max(result.shape))
    next_to = spot[:longest] + [(spot[longest] + 1) % result.shape[longest]] + spot[longest + 1:]
    return result.at[tuple(spot)].set(low).at[tuple(next_to)].set(high)


def strengthened(array, key, source, target, blocks, factor):
    owner, partner = [(jnp.arange(array.shape[axis_at]) // (array.shape[axis_at] // blocks)).reshape([-1 if axis == axis_at else 1 for axis in range(array.ndim)]) for axis_at in (source, target)]
    chosen = jax.random.permutation(key, blocks)[partner]
    strong = (owner == chosen) | (owner == (partner + blocks // 2) % blocks)
    return jnp.where(strong, factor * array, array)


def level_of(own_key, extent, shards, smallest, largest):
    level, own = 1.0, jax.random.fold_in(own_key, 6)
    for position, shards_of in shards:
        heights = jnp.exp(jax.random.uniform(jax.random.fold_in(own, position), (shards_of,), jnp.float32, smallest / len(shards), largest / len(shards)))
        level = level * jnp.repeat(heights, extent[position] // shards_of).reshape([-1 if axis == position else 1 for axis in range(len(extent))])
    return level


def noise(own_key, extent, deviation, bound, cuts=(), kind=jnp.bfloat16):
    values = deviation * jax.random.normal(own_key, extent, jnp.float32)
    if cuts:
        values = values * level_of(own_key, extent, cuts, -0.22, 0.18)
    return jnp.clip(values, -bound, bound).astype(kind)


def bell_draw_with(stream_key, shape, scale, bound, cuts, heavy, kind=jnp.bfloat16):
    result = scale * jax.random.normal(stream_key, shape, jnp.float32)
    if cuts:
        result = result * level_of(stream_key, shape, cuts, -0.22, 0.18)
    return jnp.clip(strengthened(result, jax.random.fold_in(stream_key, 3), *heavy), -bound, bound).astype(kind)


def setup_inputs(seed: int = 0) -> dict:
    key_of = jax.random.split(jax.random.key(seed), 27)
    return {
        "latents": bell_draw_with(key_of[0], (BATCH, SEQ, D), 1.0, 8.0, ((0, 16),), (0, 2, 16, 2.0), jnp.float32),
        "cotangent": bell_draw_with(key_of[1], (BATCH, SEQ, D), 1.0, 8.0, ((0, 16),), (0, 2, 16, 2.0), jnp.float32),
        "timesteps": touch_ends(jax.random.randint(key_of[2], (BATCH,), 0, 1000), jax.random.fold_in(key_of[2], 1), 0, 999).astype(jnp.int32),
        "labels": touch_ends(jax.random.randint(key_of[3], (BATCH,), 0, CLASSES), jax.random.fold_in(key_of[3], 1), 0, CLASSES - 1).astype(jnp.int32),
        "label_table": noise(key_of[4], (CLASSES, D), 1.0, 6.0, (), jnp.float32),
        "modulate_w": noise(key_of[5], (D, 6, D), D ** -0.5, 0.1875, ((0, 16), (2, 2)), jnp.float32),
        "attend_w": noise(key_of[6], (D, 3, D), D ** -0.5, 0.1875, ((0, 16), (2, 2)), jnp.float32),
        "output_projection_weight": noise(key_of[7], (D, D), (D // 16) ** -0.5, 0.75, ((0, 2), (1, 16)), jnp.float32),
        "expand_w": noise(key_of[8], (D, BLOCKS, D), D ** -0.5, 0.1875, ((0, 16), (2, 2)), jnp.float32),
        "contract_w": noise(key_of[9], (BLOCKS, D, D), FF ** -0.5, 0.09375, ((1, 2), (2, 16)), jnp.float32),
        "units_bias": noise(key_of[10], (8 + BLOCKS, D), 0.3, 1.75, ((1, 2),), jnp.float32),
        "output_width_bias": noise(key_of[11], (2, D), 0.3, 1.75, (), jnp.float32),
        "modulate_mean": noise(key_of[12], (D, 6, D), (0.13 * TOKENS ** 0.5), 128.0, ((0, 16), (2, 2)), jnp.float32),
        "modulate_square": jnp.clip(jnp.exp(math.log(190.0544) - 1.4213857 * jax.random.uniform(key_of[13], (D, 6, D), jnp.float32) ** level_of(key_of[13], (D, 6, D), ((0, 16), (2, 2)), -0.2, 0.2)), 45.8752, 190.0544),
        "attend_mean": noise(key_of[14], (D, 3, D), (0.15 * TOKENS ** 0.5), 160.0, ((0, 16), (2, 2)), jnp.float32),
        "attend_square": jnp.clip(jnp.exp(math.log(262.144) - 1.3862944 * jax.random.uniform(key_of[15], (D, 3, D), jnp.float32) ** level_of(key_of[15], (D, 3, D), ((0, 16), (2, 2)), -0.2, 0.2)), 65.536, 262.144),
        "project_mean": noise(key_of[16], (D, D), (0.045 * TOKENS ** 0.5), 48.0, ((0, 2), (1, 16)), jnp.float32),
        "project_square": jnp.clip(jnp.exp(math.log(20.97152) - 1.3862944 * jax.random.uniform(key_of[17], (D, D), jnp.float32) ** level_of(key_of[17], (D, D), ((0, 2), (1, 16)), -0.2, 0.2)), 5.24288, 20.97152),
        "expand_mean": noise(key_of[18], (D, BLOCKS, D), (0.08 * TOKENS ** 0.5), 80.0, ((0, 16), (2, 2)), jnp.float32),
        "expand_square": jnp.clip(jnp.exp(math.log(65.536) - 1.3862944 * jax.random.uniform(key_of[19], (D, BLOCKS, D), jnp.float32) ** level_of(key_of[19], (D, BLOCKS, D), ((0, 16), (2, 2)), -0.2, 0.2)), 16.384, 65.536),
        "contract_mean": noise(key_of[20], (BLOCKS, D, D), (0.066 * TOKENS ** 0.5), 64.0, ((1, 2), (2, 16)), jnp.float32),
        "contract_square": jnp.clip(jnp.exp(math.log(47.18592) - 1.3862944 * jax.random.uniform(key_of[21], (BLOCKS, D, D), jnp.float32) ** level_of(key_of[21], (BLOCKS, D, D), ((1, 2), (2, 16)), -0.2, 0.2)), 11.79648, 47.18592),
        "units_mean": noise(key_of[22], (8 + BLOCKS, D), (0.11 * TOKENS ** 0.5), 128.0, ((1, 2),), jnp.float32),
        "units_square": jnp.clip(jnp.exp(math.log(131.072) - 1.3862944 * jax.random.uniform(key_of[23], (8 + BLOCKS, D), jnp.float32) ** level_of(key_of[23], (8 + BLOCKS, D), ((1, 2),), -0.2, 0.2)), 32.768, 131.072),
        "widths_mean": noise(key_of[24], (2, D), (0.11 * TOKENS ** 0.5), 128.0, (), jnp.float32),
        "widths_square": jnp.clip(jnp.exp(jax.random.uniform(key_of[25], (2, D), jnp.float32, math.log(32.768), math.log(131.072))), 32.768, 131.072),
    }


@jax.custom_vjp
def reduced_precision(v):
    return lax.optimization_barrier(v.astype(jnp.bfloat16)).astype(jnp.float32)

@jax.custom_vjp
def reduced_backward(v):
    return v

def low_keep(v):
    return (reduced_precision(v), None)

def low_pass(kept, grad):
    return (grad,)

def back_keep(v):
    return (v, None)

def back_low(kept, grad):
    return (reduced_precision(grad),)
reduced_precision.defvjp(low_keep, low_pass)
reduced_backward.defvjp(back_keep, back_low)
BETA_ONE = 0.9
BETA_TWO = 0.999
ADAM_EPS = 1e-08
NORM_EPS = 1e-06
EXACT_PRECISION = lax.Precision.HIGHEST

def frequencies(stamps, features):
    half_count = features // 2
    freq_index = jnp.arange(half_count, dtype=jnp.float32)
    freq_rates = jnp.exp(freq_index * (-math.log(10000.0) / half_count))
    angles = stamps.astype(jnp.float32)[:, None] * freq_rates[None, :]
    return jnp.concatenate([jnp.cos(angles), jnp.sin(angles)], axis=1)

def normalize(rows_in):
    centred = rows_in - lax.optimization_barrier(jnp.mean(rows_in, axis=-1, keepdims=True))
    inverse = lax.rsqrt(lax.optimization_barrier(jnp.mean(jnp.square(centred), axis=-1, keepdims=True)) + NORM_EPS)
    return centred * inverse

def forward(params, latents, condition):
    modulate_w, attend_w, output_projection_weight, expand_w, contract_w, units_bias, output_width_bias = params
    latent_count, length, features = latents.shape
    activated = reduced_precision(jax.nn.silu(condition))
    modulation = reduced_backward(jnp.einsum('ld,dkf->lkf', activated, reduced_precision(modulate_w), precision=EXACT_PRECISION) + units_bias[:6][None])
    pieces = [modulation[:, part_index][:, None, :] for part_index in range(6)]
    shift_one, scale_one, gate_one, shift_two, scale_two, gate_two = pieces
    normed_one = normalize(latents)
    input_one = reduced_precision(normed_one * (1.0 + scale_one) + shift_one)
    projected = jnp.einsum('lsd,dkf->lskf', input_one, reduced_precision(attend_w), precision=EXACT_PRECISION)
    head_shape = (latent_count, length, HEADS, HEAD_DIM)
    query_heads = reduced_precision(reduced_backward(projected[:, :, 0] + units_bias[6])).reshape(head_shape)
    key_heads = reduced_precision(reduced_backward(projected[:, :, 1])).reshape(head_shape)
    value_heads = reduced_precision(reduced_backward(projected[:, :, 2] + units_bias[7])).reshape(head_shape)
    scores = reduced_backward(jnp.einsum('lqhe,lkhe->lhqk', query_heads, key_heads, precision=EXACT_PRECISION) * HEAD_DIM ** (-0.5))
    attn_probs = reduced_precision(jax.nn.softmax(scores, axis=-1))
    merged_head_values = jnp.einsum('lhqk,lkhe->lqhe', attn_probs, value_heads, precision=EXACT_PRECISION)
    merged_head_values = reduced_precision(reduced_backward(merged_head_values.reshape(latent_count, length, features)))
    attention_output = reduced_backward(jnp.einsum('aob,bx->aox', merged_head_values, reduced_precision(output_projection_weight), precision=EXACT_PRECISION) + output_width_bias[0])
    after_attn = latents + gate_one * attention_output
    normed_two = normalize(after_attn)
    input_two = reduced_precision(normed_two * (1.0 + scale_two) + shift_two)
    hidden_pre = reduced_backward(jnp.einsum('lsd,djf->lsjf', input_two, reduced_precision(expand_w), precision=EXACT_PRECISION) + units_bias[8:])
    hidden = reduced_precision(jax.nn.gelu(hidden_pre, approximate=True))
    contracted = reduced_backward(jnp.einsum('lsjf,jfe->lse', hidden, reduced_precision(contract_w), precision=EXACT_PRECISION) + output_width_bias[1])
    return after_attn + gate_two * contracted

def adam(weight, first_old, second_old, upstream, step_rate):
    first_new = BETA_ONE * first_old + (1.0 - BETA_ONE) * upstream
    second_new = BETA_TWO * second_old + (1.0 - BETA_TWO) * upstream * upstream
    fixed_first = first_new / (1.0 - BETA_ONE ** STEP)
    fixed_second = second_new / (1.0 - BETA_TWO ** STEP)
    return (first_new, second_new, weight - step_rate * fixed_first / (jnp.sqrt(fixed_second) + ADAM_EPS))

def grouped(array_in):
    return array_in.reshape((N_DP, array_in.shape[0] // N_DP) + array_in.shape[1:])

def reference(latents, cotangent, timesteps, labels, label_table, modulate_w, attend_w, output_projection_weight, expand_w, contract_w, units_bias, output_width_bias, modulate_mean, modulate_square, attend_mean, attend_square, project_mean, project_square, expand_mean, expand_square, contract_mean, contract_square, units_mean, units_square, widths_mean, widths_square):
    condition = jnp.take(label_table, labels, axis=0) + frequencies(timesteps, D)
    params = (modulate_w, attend_w, output_projection_weight, expand_w, contract_w, units_bias, output_width_bias)

    def group_step(totals, inputs):
        latent_block, cond_block, cot_block = inputs
        output, pullback = jax.vjp(forward, params, latent_block, cond_block)
        grads, latent_grad, cond_part = pullback(cot_block)
        totals = jax.tree.map(jnp.add, totals, grads)
        return (totals, (output, latent_grad, cond_part))
    zeros = jax.tree.map(jnp.zeros_like, params)
    totals, (outputs, latent_grads, cond_parts) = lax.scan(group_step, zeros, (grouped(latents), grouped(condition), grouped(cotangent)))
    block_out = outputs.reshape(latents.shape)
    latents_grad = latent_grads.reshape(latents.shape)
    cond_grad = cond_parts.reshape(condition.shape)
    g_mod, g_att, g_proj, g_exp, g_con, g_units, g_widths = totals
    m_mod, s_mod, n_mod = adam(modulate_w, modulate_mean, modulate_square, g_mod, D ** (-0.5))
    m_att, s_att, n_att = adam(attend_w, attend_mean, attend_square, g_att, D ** (-0.5))
    m_proj, s_proj, n_proj = adam(output_projection_weight, project_mean, project_square, g_proj, (D // 16) ** (-0.5))
    m_exp, s_exp, n_exp = adam(expand_w, expand_mean, expand_square, g_exp, D ** (-0.5))
    m_con, s_con, n_con = adam(contract_w, contract_mean, contract_square, g_con, FF ** (-0.5))
    m_units, s_units, n_units = adam(units_bias, units_mean, units_square, g_units, 0.15)
    m_widths, s_widths, n_widths = adam(output_width_bias, widths_mean, widths_square, g_widths, 0.15)
    return (block_out, latents_grad, cond_grad, g_mod, m_mod, s_mod, n_mod, g_att, m_att, s_att, n_att, g_proj, m_proj, s_proj, n_proj, g_exp, m_exp, s_exp, n_exp, g_con, m_con, s_con, n_con, g_units, m_units, s_units, n_units, g_widths, m_widths, s_widths, n_widths)
```

```python
import math

import jax
import jax.numpy as jnp
from jax import lax
from jax.experimental import pallas as pl
from jax.experimental.pallas import tpu as pltpu
from jax.sharding import PartitionSpec as P

D = 1152
HEAD_DIM = 72
FF = 4608
STEP = 10


BETA_ONE = 0.9
BETA_TWO = 0.999
ADAM_EPS = 1e-08
NORM_EPS = 1e-06
EXACT_PRECISION = lax.Precision.HIGHEST


def frequencies(stamps, features):
    half_count = features // 2
    freq_index = jnp.arange(half_count, dtype=jnp.float32)
    freq_rates = jnp.exp(freq_index * (-math.log(10000.0) / half_count))
    angles = stamps.astype(jnp.float32)[:, None] * freq_rates[None, :]
    return jnp.concatenate([jnp.cos(angles), jnp.sin(angles)], axis=1)


def normalize(rows_in):
    centred = rows_in - jnp.mean(rows_in, axis=-1, keepdims=True)
    inverse = lax.rsqrt(jnp.mean(jnp.square(centred), axis=-1, keepdims=True) + NORM_EPS)
    return (centred * inverse, inverse)


def norm_back(normed, inverse, upstream):
    return inverse * (
        upstream
        - jnp.mean(upstream, axis=-1, keepdims=True)
        - normed * jnp.mean(upstream * normed, axis=-1, keepdims=True)
    )


def gelu_tanh(rows_in):
    return jax.nn.gelu(rows_in, approximate=True)


def local_grad(mapping, rows_in, upstream):
    return jax.vjp(mapping, rows_in)[1](upstream)[0]


def adam(weight, first_old, second_old, upstream, step_rate):
    first_new = BETA_ONE * first_old + (1.0 - BETA_ONE) * upstream
    second_new = BETA_TWO * second_old + (1.0 - BETA_TWO) * upstream * upstream
    fixed_first = first_new / (1.0 - BETA_ONE**STEP)
    fixed_second = second_new / (1.0 - BETA_TWO**STEP)
    return (
        first_new,
        second_new,
        weight - step_rate * fixed_first / (jnp.sqrt(fixed_second) + ADAM_EPS),
    )


GROUPS = 2
VMEM_ASK = 48 * 1024 * 1024


def swap(piece):
    return lax.ppermute(piece, "tensor", [(0, 1), (1, 0)])


def pair_sum(part):
    return part.astype(jnp.float32) + swap(part).astype(jnp.float32)


def rows_dot(left, right):
    return lax.dot_general(
        left, right, (((1,), (0,)), ((), ())), preferred_element_type=jnp.float32
    )


def lanes_dot(left, right):
    return lax.dot_general(
        left, right, (((1,), (1,)), ((), ())), preferred_element_type=jnp.float32
    )


def tall_dot(left, right):
    return lax.dot_general(
        left, right, (((0,), (0,)), ((), ())), preferred_element_type=jnp.float32
    )


def head_probs(query, key):
    scores = lanes_dot(query, key) * (HEAD_DIM ** (-0.5))
    raised = jnp.exp(scores - jnp.max(scores, axis=-1, keepdims=True))
    return raised * (1.0 / jnp.sum(raised, axis=-1, keepdims=True))


def attend_kernel(qkv_ref, mixed_ref):
    width = mixed_ref.shape[-1]
    outs = []
    for head in range(width // HEAD_DIM):
        at = head * HEAD_DIM
        query = qkv_ref[0, :, at : at + HEAD_DIM]
        key = qkv_ref[0, :, width + at : width + at + HEAD_DIM]
        value = qkv_ref[0, :, 2 * width + at : 2 * width + at + HEAD_DIM]
        probs = head_probs(query, key).astype(jnp.bfloat16)
        outs.append(rows_dot(probs, value))
    mixed_ref[0] = jnp.concatenate(outs, axis=1).astype(jnp.bfloat16)


def attend_back_kernel(qkv_ref, up_ref, grad_ref):
    width = up_ref.shape[-1]
    score_scale = HEAD_DIM ** (-0.5)
    queries, keys, values = [], [], []
    for head in range(width // HEAD_DIM):
        at = head * HEAD_DIM
        query = qkv_ref[0, :, at : at + HEAD_DIM]
        key = qkv_ref[0, :, width + at : width + at + HEAD_DIM]
        value = qkv_ref[0, :, 2 * width + at : 2 * width + at + HEAD_DIM]
        upstream = up_ref[0, :, at : at + HEAD_DIM]
        probs = head_probs(query, key)
        values.append(tall_dot(probs.astype(jnp.bfloat16), upstream))
        probs_grad = lanes_dot(upstream, value)
        scores_grad = (
            probs * (probs_grad - jnp.sum(probs * probs_grad, axis=-1, keepdims=True))
        ).astype(jnp.bfloat16)
        queries.append(rows_dot(scores_grad, key) * score_scale)
        keys.append(tall_dot(scores_grad, query) * score_scale)
    grad_ref[0] = jnp.concatenate(queries + keys + values, axis=1).astype(jnp.bfloat16)


def per_latent(kernel, out_width, flops, *arrays):
    count, length = arrays[0].shape[:2]
    moved = sum(array.size for array in arrays) + count * length * out_width
    return pl.pallas_call(
        kernel,
        grid=(count,),
        out_shape=jax.ShapeDtypeStruct((count, length, out_width), jnp.bfloat16),
        in_specs=[
            pl.BlockSpec((1, length, array.shape[2]), lambda at: (at, 0, 0)) for array in arrays
        ],
        out_specs=pl.BlockSpec((1, length, out_width), lambda at: (at, 0, 0)),
        compiler_params=pltpu.CompilerParams(vmem_limit_bytes=VMEM_ASK),
        cost_estimate=pl.CostEstimate(
            flops=flops, bytes_accessed=2 * moved, transcendentals=count * length * length * 8
        ),
    )(*arrays)


def on_device(
    latents,
    cotangent,
    timesteps,
    labels,
    label_table,
    modulate_w,
    attend_w,
    output_projection_weight,
    expand_w,
    contract_w,
    units_bias,
    output_width_bias,
    modulate_mean,
    modulate_square,
    attend_mean,
    attend_square,
    project_mean,
    project_square,
    expand_mean,
    expand_square,
    contract_mean,
    contract_square,
    units_mean,
    units_square,
    widths_mean,
    widths_square,
):
    latent_count, length, features = latents.shape
    half_width = attend_w.shape[2]
    blocks = expand_w.shape[1]
    own_rows = attend_w.shape[0]
    hidden_units = blocks * half_width
    groups = GROUPS if latent_count % GROUPS == 0 else 1
    group_latents = latent_count // groups
    tokens = group_latents * length
    half_here = lax.axis_index("tensor")
    row_start = lax.axis_index("dp") * own_rows

    attend_rows = attend_w.astype(jnp.bfloat16).reshape(own_rows, 3 * half_width)
    project_rows = output_projection_weight.astype(jnp.bfloat16).T
    expand_rows = expand_w.astype(jnp.bfloat16).reshape(own_rows, hidden_units)
    contract_rows = (
        contract_w.astype(jnp.bfloat16).transpose(2, 0, 1).reshape(own_rows, hidden_units)
    )
    mod_rows = modulate_w.astype(jnp.bfloat16).reshape(own_rows, 6 * half_width)

    all_labels = lax.all_gather(labels, "dp", axis=0, tiled=True)
    all_stamps = lax.all_gather(timesteps, "dp", axis=0, tiled=True)
    own_table = lax.dynamic_slice_in_dim(label_table, row_start, own_rows, 1)
    onehot = (
        all_labels[:, None] == jnp.arange(label_table.shape[0], dtype=jnp.int32)[None, :]
    ).astype(jnp.float32)
    half_count = features // 2
    own_index = row_start + jnp.arange(own_rows, dtype=jnp.int32)
    own_rates = jnp.exp(
        (own_index % half_count).astype(jnp.float32) * (-math.log(10000.0) / half_count)
    )
    angles = all_stamps.astype(jnp.float32)[:, None] * own_rates[None, :]
    waves = jnp.where((own_index < half_count)[None, :], jnp.cos(angles), jnp.sin(angles))
    condition = jnp.dot(onehot, own_table, precision=EXACT_PRECISION) + waves
    cond_low = jax.nn.silu(condition).astype(jnp.bfloat16)
    mod_sum = lax.psum_scatter(
        rows_dot(cond_low, mod_rows), "dp", scatter_dimension=0, tiled=True
    )
    mod_half = mod_sum.reshape(latent_count, 6, half_width) + units_bias[:6][None]
    mod_other = swap(mod_half)
    modulation = jnp.where(
        half_here == 0,
        jnp.concatenate([mod_half, mod_other], axis=2),
        jnp.concatenate([mod_other, mod_half], axis=2),
    )

    full_attend = lax.all_gather(attend_rows, "dp", axis=0, tiled=True)
    full_project = lax.all_gather(project_rows, "dp", axis=0, tiled=True)
    full_expand = lax.all_gather(expand_rows, "dp", axis=0, tiled=True)
    full_contract = lax.all_gather(contract_rows, "dp", axis=0, tiled=True)
    qkv_bias = jnp.concatenate([units_bias[6], jnp.zeros_like(units_bias[6]), units_bias[7]])
    hidden_bias = units_bias[8:].reshape(hidden_units)
    attention_flops = 4 * tokens * length * half_width

    spans = [slice(g * group_latents, (g + 1) * group_latents) for g in range(groups)]
    lat = [latents[s] for s in spans]
    cot = [cotangent[s] for s in spans]
    mods = [[modulation[s, k][:, None, :] for k in range(6)] for s in spans]
    each = range(groups)

    norm_one, flat_one, qkv, mixed, attn_part = [], [], [], [], []
    for g in each:
        normed, inverse = normalize(lat[g])
        norm_one.append((normed, inverse))
        flat_one.append(
            (normed * (1.0 + mods[g][1]) + mods[g][0])
            .astype(jnp.bfloat16)
            .reshape(tokens, features)
        )
        qkv.append(
            (rows_dot(flat_one[g], full_attend) + qkv_bias)
            .astype(jnp.bfloat16)
            .reshape(group_latents, length, 3 * half_width)
        )
        mixed.append(
            per_latent(attend_kernel, half_width, attention_flops, qkv[g]).reshape(
                tokens, half_width
            )
        )
        attn_part.append(lanes_dot(mixed[g], full_project).astype(jnp.bfloat16))
    attn_sum = [pair_sum(attn_part[g]) for g in each]

    group_shape = (group_latents, length, features)
    attention_output, after_attn, norm_two, input_two = [], [], [], []
    mlp_part, contract_in, hidden_low, expand_in, input_two_part = [], [], [], [], []
    for g in each:
        attention_output.append((attn_sum[g] + output_width_bias[0]).reshape(group_shape))
        after_attn.append(lat[g] + mods[g][2] * attention_output[g])
        normed, inverse = normalize(after_attn[g])
        norm_two.append((normed, inverse))
        input_two.append(
            (normed * (1.0 + mods[g][4]) + mods[g][3])
            .astype(jnp.bfloat16)
            .reshape(tokens, features)
        )
        hidden_pre = rows_dot(input_two[g], full_expand) + hidden_bias
        hidden_low.append(gelu_tanh(hidden_pre).astype(jnp.bfloat16))
        contract_in.append((mods[g][5] * cot[g]).astype(jnp.bfloat16).reshape(tokens, features))
        hidden_grad = rows_dot(contract_in[g], full_contract)
        expand_in.append(local_grad(gelu_tanh, hidden_pre, hidden_grad).astype(jnp.bfloat16))
        input_two_part.append(lanes_dot(expand_in[g], full_expand).astype(jnp.bfloat16))
        mlp_part.append(lanes_dot(hidden_low[g], full_contract).astype(jnp.bfloat16))
    input_two_sum = [pair_sum(input_two_part[g]) for g in each]
    mlp_sum = [pair_sum(mlp_part[g]) for g in each]

    def summed_grad(lefts, rights):
        total = tall_dot(lefts[0], rights[0])
        for g in range(1, groups):
            total = total + tall_dot(lefts[g], rights[g])
        return total.astype(jnp.bfloat16)

    def scattered(local):
        return lax.psum_scatter(local, "dp", scatter_dimension=0, tiled=True).astype(jnp.float32)

    contract_own = scattered(summed_grad(contract_in, hidden_low))
    expand_own = scattered(summed_grad(input_two, expand_in))

    after_grad, attn_in, qkv_grad, input_one_part = [], [], [], []
    scale_two_grad, shift_two_grad, gate_one_grad = [], [], []
    for g in each:
        normed, inverse = norm_two[g]
        upstream = input_two_sum[g].reshape(group_shape)
        scale_two_grad.append(jnp.sum(upstream * normed, axis=1))
        shift_two_grad.append(jnp.sum(upstream, axis=1))
        after_grad.append(cot[g] + norm_back(normed, inverse, upstream * (1.0 + mods[g][4])))
        gate_one_grad.append(jnp.sum(after_grad[g] * attention_output[g], axis=1))
        attn_in.append(
            (mods[g][2] * after_grad[g]).astype(jnp.bfloat16).reshape(tokens, features)
        )
        mixed_grad = (
            rows_dot(attn_in[g], full_project)
            .astype(jnp.bfloat16)
            .reshape(group_latents, length, half_width)
        )
        qkv_grad.append(
            per_latent(
                attend_back_kernel, 3 * half_width, 3 * attention_flops, qkv[g], mixed_grad
            ).reshape(tokens, 3 * half_width)
        )
        input_one_part.append(lanes_dot(qkv_grad[g], full_attend).astype(jnp.bfloat16))
    input_one_sum = [pair_sum(input_one_part[g]) for g in each]
    project_own = scattered(summed_grad(attn_in, mixed))
    attend_own = scattered(summed_grad(flat_one, qkv_grad))

    block_out, gate_two_grad, latents_grad, scale_one_grad, shift_one_grad = [], [], [], [], []
    for g in each:
        contracted = (mlp_sum[g] + output_width_bias[1]).reshape(group_shape)
        block_out.append(after_attn[g] + mods[g][5] * contracted)
        gate_two_grad.append(jnp.sum(cot[g] * contracted, axis=1))
    for g in each:
        normed, inverse = norm_one[g]
        upstream = input_one_sum[g].reshape(group_shape)
        scale_one_grad.append(jnp.sum(upstream * normed, axis=1))
        shift_one_grad.append(jnp.sum(upstream, axis=1))
        latents_grad.append(
            after_grad[g] + norm_back(normed, inverse, upstream * (1.0 + mods[g][1]))
        )
    block_out = jnp.concatenate(block_out, axis=0)
    latents_grad = jnp.concatenate(latents_grad, axis=0)

    mod_grad = jnp.stack(
        [
            jnp.concatenate(piece, axis=0)
            for piece in (
                shift_one_grad,
                scale_one_grad,
                gate_one_grad,
                shift_two_grad,
                scale_two_grad,
                gate_two_grad,
            )
        ],
        axis=1,
    ).astype(jnp.bfloat16)
    mod_grad_half = lax.dynamic_slice_in_dim(mod_grad, half_here * half_width, half_width, 2)
    all_mod_grad = lax.all_gather(
        mod_grad_half.reshape(latent_count, 6 * half_width), "dp", axis=0, tiled=True
    )
    modulate_grad = tall_dot(cond_low, all_mod_grad).reshape(own_rows, 6, half_width)
    cond_sum = pair_sum(lanes_dot(all_mod_grad, mod_rows).astype(jnp.bfloat16))
    cond_own = local_grad(jax.nn.silu, condition, cond_sum)
    cond_grad = lax.all_to_all(cond_own, "dp", split_axis=0, concat_axis=1, tiled=True)

    def token_sum(pieces):
        return sum(jnp.sum(piece, axis=0, dtype=jnp.float32) for piece in pieces)

    qkv_bias_grad = token_sum(qkv_grad)
    bias_local = jnp.concatenate(
        [
            qkv_bias_grad[:half_width],
            qkv_bias_grad[2 * half_width :],
            token_sum(expand_in),
            token_sum(attn_in),
            token_sum(contract_in),
        ]
    )
    bias_sum = jnp.sum(lax.all_gather(bias_local[None], "dp", axis=0, tiled=True), axis=0)
    split_at = (2 + blocks) * half_width
    units_grad = jnp.concatenate(
        [
            jnp.sum(all_mod_grad, axis=0, dtype=jnp.float32).reshape(6, half_width),
            bias_sum[:split_at].reshape(2 + blocks, half_width),
        ],
        axis=0,
    )
    widths_grad = bias_sum[split_at:].reshape(2, features)
    attend_grad = attend_own.reshape(own_rows, 3, half_width)
    project_grad = project_own.T
    expand_grad = expand_own.reshape(own_rows, blocks, half_width)
    contract_grad = contract_own.reshape(own_rows, blocks, half_width).transpose(1, 2, 0)

    m_mod, s_mod, n_mod = adam(
        modulate_w, modulate_mean, modulate_square, modulate_grad, D ** (-0.5)
    )
    m_att, s_att, n_att = adam(attend_w, attend_mean, attend_square, attend_grad, D ** (-0.5))
    m_proj, s_proj, n_proj = adam(
        output_projection_weight, project_mean, project_square, project_grad, (D // 16) ** (-0.5)
    )
    m_exp, s_exp, n_exp = adam(expand_w, expand_mean, expand_square, expand_grad, D ** (-0.5))
    m_con, s_con, n_con = adam(
        contract_w, contract_mean, contract_square, contract_grad, FF ** (-0.5)
    )
    m_units, s_units, n_units = adam(units_bias, units_mean, units_square, units_grad, 0.15)
    m_widths, s_widths, n_widths = adam(
        output_width_bias, widths_mean, widths_square, widths_grad, 0.15
    )
    return (
        block_out,
        latents_grad,
        cond_grad,
        modulate_grad,
        m_mod,
        s_mod,
        n_mod,
        attend_grad,
        m_att,
        s_att,
        n_att,
        project_grad,
        m_proj,
        s_proj,
        n_proj,
        expand_grad,
        m_exp,
        s_exp,
        n_exp,
        contract_grad,
        m_con,
        s_con,
        n_con,
        units_grad,
        m_units,
        s_units,
        n_units,
        widths_grad,
        m_widths,
        s_widths,
        n_widths,
    )


def solution(mesh):
    placed = (
        P("dp", None, None),
        P("dp", None, None),
        P("dp"),
        P("dp"),
        P(),
        P("dp", None, "tensor"),
        P("dp", None, "tensor"),
        P("tensor", "dp"),
        P("dp", None, "tensor"),
        P(None, "tensor", "dp"),
        P(None, "tensor"),
        P(),
        P("dp", None, "tensor"),
        P("dp", None, "tensor"),
        P("dp", None, "tensor"),
        P("dp", None, "tensor"),
        P("tensor", "dp"),
        P("tensor", "dp"),
        P("dp", None, "tensor"),
        P("dp", None, "tensor"),
        P(None, "tensor", "dp"),
        P(None, "tensor", "dp"),
        P(None, "tensor"),
        P(None, "tensor"),
        P(),
        P(),
    )
    return jax.shard_map(
        on_device,
        mesh=mesh,
        in_specs=placed,
        out_specs=(
            P("dp", None, None),
            P("dp", None, None),
            P("dp", None),
            P("dp", None, "tensor"),
            P("dp", None, "tensor"),
            P("dp", None, "tensor"),
            P("dp", None, "tensor"),
            P("dp", None, "tensor"),
            P("dp", None, "tensor"),
            P("dp", None, "tensor"),
            P("dp", None, "tensor"),
            P("tensor", "dp"),
            P("tensor", "dp"),
            P("tensor", "dp"),
            P("tensor", "dp"),
            P("dp", None, "tensor"),
            P("dp", None, "tensor"),
            P("dp", None, "tensor"),
            P("dp", None, "tensor"),
            P(None, "tensor", "dp"),
            P(None, "tensor", "dp"),
            P(None, "tensor", "dp"),
            P(None, "tensor", "dp"),
            P(None, "tensor"),
            P(None, "tensor"),
            P(None, "tensor"),
            P(None, "tensor"),
            P(),
            P(),
            P(),
            P(),
        ),
        check_vma=False,
    )
```
